32 devices in a mesh: ctx: 16 (over z, y, x), head: 2 (over core).
Axes of the slice: x: 2, y: 2, z: 4, core: 2. Of those that a mesh axis runs over, the one named last changes fastest.
Arguments:
- queries: bfloat16 [6144, 4096], P('ctx', 'head'), may hold values from -200 to 200
- key_matrix: bfloat16 [6144, 1024], P('ctx', 'head'), may hold values from -6 to 6
- value_matrix: bfloat16 [6144, 1024], P('ctx', 'head'), may hold values from -6 to 6
- doc_ids: int32 [6144], P('ctx'), may hold values from 0 to 7, never falling along the last dimension, each value on 1 to 3456 neighbouring positions
- out_weight: bfloat16 [4096, 4096], P('head'), may hold values from -0.09375 to 0.09375
Outputs:
- projected: bfloat16 [6144, 4096], P(('ctx', 'head'))
The draws below stay inside these ranges and needn't reach their ends.
Inputs may be any that keep to these rules, and one draw needn't show every extreme that they name: `doc_ids`: document ids never fall along the tokens; each document has 1 to 3456 tokens and one has exactly 3456.
All inputs are finite; a program needn't handle non-finite values.
Results may differ from the reference program's by a relative error of at most 0.019.
Values may be sent and summed in bfloat16 or wider, within the bound.
A program may use at most 256 MiB of HBM per device.

```python
import math
import jax
import jax.numpy as jnp
import numpy as np
from jax import lax

D = 4096
QUERY_HEADS = 32
KEY_VALUE_HEADS = 8
HEAD_WIDTH = 128
PACKED_TOKENS = 6144
MOST = 3456
DOCS = 8


def make_pair(key):
    base_key = jax.random.fold_in(key, 11)
    key_query, key_random_seeds = jax.random.split(base_key, 2)
    query_draw = jnp.clip(jax.random.normal(key_query, (PACKED_TOKENS, QUERY_HEADS * HEAD_WIDTH), jnp.float32), -6.0, 6.0)
    key_sample = jnp.clip(jax.random.normal(key_random_seeds, (PACKED_TOKENS, KEY_VALUE_HEADS * HEAD_WIDTH), jnp.float32), -6.0, 6.0)
    return (query_draw, key_sample)


def draw_queries(key, part):
    return make_pair(key)[0].astype(jnp.bfloat16)


def draw_key_matrix(key, part):
    return make_pair(key)[1].astype(jnp.bfloat16)


def level_of(rng, dims, cuts, least, high):
    gain, own = 1.0, jax.random.fold_in(rng, 6)
    for position, shards_of in cuts:
        draws = jnp.exp(jax.random.uniform(jax.random.fold_in(own, position), (shards_of,), jnp.float32, least / len(cuts), high / len(cuts)))
        gain = gain * jnp.repeat(draws, dims[position] // shards_of).reshape([-1 if axis == position else 1 for axis in range(len(dims))])
    return gain


def length_profile(count, total, bound, lean):
    portions = [(1 << 20) // math.isqrt(standing ** lean) + 1 for standing in range(2, count + 1)]
    spare, given = total - bound - (count - 1), [1] * (count - 1)
    while spare > 0:
        movable = [i for i in range(count - 1) if given[i] < bound]
        pool, remaining = sum([portions[i] for i in movable]), spare
        for i in movable:
            addition = min(bound - given[i], max(1, remaining * portions[i] // pool), spare)
            given[i] = given[i] + addition
            spare = spare - addition
    return np.array([bound] + given)


def uneven_parts(rng, number_of, total, most, lean):
    if number_of == 2:
        one = jax.random.randint(rng, (), max(1, total - most), min(most, total - 1) + 1)
        return jnp.stack([one, total - one])
    sizes = jnp.asarray(length_profile(number_of, total, most, lean), jnp.int32)
    twos = (number_of - 1) // 2
    source_of, sink = sizes[1:1 + 2 * twos:2], sizes[2:2 + 2 * twos:2]
    room = jnp.minimum(source_of - 1, most - sink)
    shifted = jax.random.randint(jax.random.fold_in(rng, 1), (twos,), 0, 1 << 20) % (room + 1)
    sizes = sizes.at[1:1 + 2 * twos:2].set(source_of - shifted).at[2:2 + 2 * twos:2].set(sink + shifted)
    return sizes[jax.random.permutation(jax.random.fold_in(rng, 2), number_of)]


def normal_values(stream_key, shape, spread, bound, pieces=(), kind=jnp.bfloat16):
    array = jax.random.normal(stream_key, shape, jnp.float32) * spread
    if len(pieces) > 0:
        array = level_of(stream_key, shape, pieces, -0.22, 0.18) * array
    return jnp.clip(array, min=-bound, max=bound).astype(kind)


def setup_inputs(seed: int = 0) -> dict:
    keys = jax.random.split(jax.random.key(seed), 6)
    return {
        "queries": draw_queries(jax.random.fold_in(keys[5], 71), 0),
        "key_matrix": draw_key_matrix(jax.random.fold_in(keys[5], 71), 0),
        "value_matrix": normal_values(keys[2], (PACKED_TOKENS, KEY_VALUE_HEADS * HEAD_WIDTH), 1.0, 6.0, ((0, 16), (1, 2))),
        "doc_ids": jnp.searchsorted(jnp.cumsum(uneven_parts(keys[3], DOCS, PACKED_TOKENS, MOST, 2)), jnp.arange(PACKED_TOKENS), side="right").astype(jnp.int32),
        "out_weight": normal_values(keys[4], (QUERY_HEADS * HEAD_WIDTH, D), (QUERY_HEADS * HEAD_WIDTH) ** -0.5, 0.09375, ((0, 2),)),
    }


def reference(queries, key_matrix, value_matrix, doc_ids, out_weight):
    queries_per_group = QUERY_HEADS // KEY_VALUE_HEADS
    query_heads = queries.reshape(PACKED_TOKENS, QUERY_HEADS, HEAD_WIDTH)
    key_head_split = key_matrix.reshape(PACKED_TOKENS, KEY_VALUE_HEADS, HEAD_WIDTH)
    value_head_split = value_matrix.reshape(PACKED_TOKENS, KEY_VALUE_HEADS, HEAD_WIDTH)
    positions = jnp.arange(PACKED_TOKENS, dtype=jnp.int32)
    allowed = (doc_ids[:, None] == doc_ids[None, :]) & (positions[:, None] >= positions[None, :])
    score_scale = HEAD_WIDTH ** -0.5

    def one_head(head_index):
        kv_index = head_index // queries_per_group
        query_head = lax.dynamic_index_in_dim(query_heads, head_index, 1, False)
        key_head = lax.dynamic_index_in_dim(key_head_split, kv_index, 1, False)
        value_head = lax.dynamic_index_in_dim(value_head_split, kv_index, 1, False)
        scores = jnp.dot(query_head, key_head.T, preferred_element_type=jnp.float32) * score_scale
        scores = jnp.where(allowed, scores, jnp.float32(-1e30))
        row_max = jnp.max(scores, axis=1)
        weights = jnp.where(allowed, jnp.exp(scores - row_max[:, None]), jnp.float32(0.0))
        denominator = jnp.sum(weights, axis=1)
        weighted = jnp.dot(weights.astype(jnp.bfloat16), value_head, preferred_element_type=jnp.float32)
        return (weighted / denominator[:, None]).astype(jnp.bfloat16)

    per_head = lax.map(one_head, jnp.arange(QUERY_HEADS, dtype=jnp.int32))
    attended = jnp.transpose(per_head, (1, 0, 2)).reshape(PACKED_TOKENS, QUERY_HEADS * HEAD_WIDTH)
    return jnp.dot(attended, out_weight, preferred_element_type=jnp.float32).astype(jnp.bfloat16)
```

```python
import functools
import jax
import jax.numpy as jnp
from jax import lax
from jax.experimental import pallas as pl
from jax.experimental.pallas import tpu as pltpu
from jax.sharding import PartitionSpec as P

HEAD_WIDTH = 128


def gathered_attention(queries, key_matrix, value_matrix, doc_ids, out_weight):
    tok_rows = queries.shape[0]
    kv_here = key_matrix.shape[1] // HEAD_WIDTH
    queries_per_group = queries.shape[1] // key_matrix.shape[1]
    all_rows = queries_per_group * tok_rows
    my_index = lax.axis_index("ctx")
    q_pos = my_index * tok_rows + jnp.arange(tok_rows, dtype=jnp.int32)
    q_rows = (
        queries.reshape(tok_rows, kv_here, queries_per_group, HEAD_WIDTH)
        .transpose(1, 2, 0, 3)
        .reshape(kv_here, all_rows, HEAD_WIDTH)
    )
    score_scale = HEAD_WIDTH ** (-0.5)
    running = jnp.full((kv_here, all_rows), -1e30, jnp.float32)
    part_keys = lax.all_gather(key_matrix, "ctx", axis=0, tiled=True)
    part_values = lax.all_gather(value_matrix, "ctx", axis=0, tiled=True)
    part_docs = lax.all_gather(doc_ids, "ctx", axis=0, tiled=True)
    key_count = part_keys.shape[0]
    k_pos = jnp.arange(key_count, dtype=jnp.int32)
    keys_three = part_keys.reshape(key_count, kv_here, HEAD_WIDTH).transpose(1, 0, 2)
    values_three = part_values.reshape(key_count, kv_here, HEAD_WIDTH).transpose(1, 0, 2)
    scores = (
        jnp.einsum("hqd,hkd->hqk", q_rows, keys_three, preferred_element_type=jnp.float32)
        * score_scale
    )
    allowed = (
        (doc_ids[:, None] == part_docs[None, :])
        & (q_pos[:, None] >= k_pos[None, :])
        & (k_pos[None, :] >= 0)
    )
    allowed = jnp.tile(allowed, (queries_per_group, 1))[None]
    scores = jnp.where(allowed, scores, jnp.float32(-1e30))
    new_max = jnp.maximum(running, jnp.max(scores, axis=-1))
    weights = jnp.where(allowed, jnp.exp(scores - new_max[..., None]), jnp.float32(0.0))
    denominator = jnp.sum(weights, axis=-1)
    weighted = jnp.einsum(
        "hqk,hkd->hqd",
        weights.astype(jnp.bfloat16),
        values_three,
        preferred_element_type=jnp.float32,
    )
    running_state = (new_max, denominator, weighted)
    running, denominator, weighted = running_state
    attended = (weighted / denominator[..., None]).astype(jnp.bfloat16)
    attended = (
        attended.reshape(kv_here, queries_per_group, tok_rows, HEAD_WIDTH)
        .transpose(2, 0, 1, 3)
        .reshape(tok_rows, kv_here * queries_per_group * HEAD_WIDTH)
    )
    return lax.psum_scatter(
        jnp.dot(attended, out_weight, preferred_element_type=jnp.float32).astype(jnp.bfloat16),
        "head",
        scatter_dimension=0,
        tiled=True,
    )


NEG = -1e30
LOG2E = 1.4426950408889634
PLANE = 4
REACH = 9
SLOTS = REACH + 1
OUT_TILE = 512


def fused_kernel(
    q_ref, k_ref, v_ref, qdoc_ref, kdoc_ref, w_hbm, out_ref,
    kv, docs, bias, m_s, l_s, acc, att, w_vm, part, theirs, swapped,
    send_sem, recv_sem, dsend_sem, drecv_sem, w_sem, osend_sem, orecv_sem,
):
    tok = q_ref.shape[0]
    heads = k_ref.shape[1] // HEAD_WIDTH
    group = q_ref.shape[1] // k_ref.shape[1]
    me = lax.axis_index("ctx")
    core = lax.axis_index("head")
    z, y, x = me // PLANE, (me // 2) % 2, me % 2
    dx, dy = 1 - 2 * x, 2 - 4 * y
    x_src = (4 * x, 4 + 4 * x, 2 + 4 * (1 - x) * (1 - y))
    y_src = (4 * y, 4 + 4 * y, 3 + 4 * y + x * (2 - 4 * y))
    z_src = (0, 4, 5)
    planes = lax.axis_size("ctx") // PLANE
    links = (
        (x_src, dx, None),
        (y_src, dy, None),
        (z_src, PLANE, z < planes - 1),
    )

    barrier = pltpu.get_barrier_semaphore()
    pl.semaphore_signal(barrier, inc=1, device_id={"ctx": me + dx})
    pl.semaphore_signal(barrier, inc=1, device_id={"ctx": me + dy})
    pl.semaphore_signal(barrier, inc=1, device_id={"head": 1 - core})

    @pl.when(z < planes - 1)
    def _():
        pl.semaphore_signal(barrier, inc=1, device_id={"ctx": me + PLANE})

    @pl.when(z > 0)
    def _():
        pl.semaphore_signal(barrier, inc=1, device_id={"ctx": me - PLANE})

    weight_copy = pltpu.make_async_copy(w_hbm, w_vm, w_sem)
    weight_copy.start()
    for h in range(heads):
        columns = pl.ds(h * HEAD_WIDTH, HEAD_WIDTH)
        kv[0, h, 0] = k_ref[:, columns]
        kv[0, h, 1] = v_ref[:, columns]
    docs[0] = kdoc_ref[...]

    peers = 3 + jnp.where(z > 0, 1, 0) + jnp.where(z < planes - 1, 1, 0)
    pl.semaphore_wait(barrier, peers)

    def chunk_copy(link, s, h):
        step = links[link][1]
        return pltpu.make_async_remote_copy(
            src_ref=kv.at[s, h],
            dst_ref=kv.at[s + step, h],
            send_sem=send_sem.at[link, s, h],
            recv_sem=recv_sem.at[s + step, h],
            device_id={"ctx": me + step},
        )

    def doc_copy(link, s):
        step = links[link][1]
        return pltpu.make_async_remote_copy(
            src_ref=docs.at[s],
            dst_ref=docs.at[s + step],
            send_sem=dsend_sem.at[link, s],
            recv_sem=drecv_sem.at[s + step],
            device_id={"ctx": me + step},
        )

    def sends(link, s):
        sources, _, also = links[link]
        here = (s == sources[0]) | (s == sources[1]) | (s == sources[2])
        if also is not None:
            here = here & also
        return here

    def forward(s, h):
        for link in (2, 0, 1):
            @pl.when(sends(link, s))
            def _():
                @pl.when(h == 0)
                def _():
                    doc_copy(link, s).start()

                chunk_copy(link, s, h).start()

    def send_own(h, carry):
        forward(jnp.int32(0), h)
        return carry

    lax.fori_loop(0, heads, send_own, 0)

    score_scale = HEAD_WIDTH ** (-0.5) * LOG2E
    lane_tiles = tok // HEAD_WIDTH

    def wide(a):
        return jnp.concatenate([a] * lane_tiles, axis=1)

    def piece(s, h, b, first):
        keys = kv[s, h, 0]
        values = kv[s, h, 1]
        for r in range(group):
            head = h * group + r
            q = q_ref[:, pl.ds(pl.multiple_of(head * HEAD_WIDTH, HEAD_WIDTH), HEAD_WIDTH)]
            scores = lax.dot_general(
                q, keys, (((1,), (1,)), ((), ())), preferred_element_type=jnp.float32
            )
            scores = scores * score_scale + bias[b]
            top = jnp.broadcast_to(
                jnp.max(scores, axis=1, keepdims=True), (tok, HEAD_WIDTH)
            )
            if not first:
                before = m_s[head]
                top = jnp.maximum(before, top)
            weights = jnp.exp2(scores - wide(top))
            total = weights[:, :HEAD_WIDTH]
            for i in range(1, lane_tiles):
                total = total + weights[:, i * HEAD_WIDTH:(i + 1) * HEAD_WIDTH]
            summed = jnp.dot(
                weights.astype(jnp.bfloat16), values, preferred_element_type=jnp.float32
            )
            if not first:
                fade = jnp.exp2(before - top)
                total = total + l_s[head] * fade
                summed = summed + acc[head] * fade
            m_s[head] = top
            l_s[head] = total
            acc[head] = summed

    def same_doc(s):
        return wide(qdoc_ref[...]) == docs[s, 0:1, :]

    rows = lax.broadcasted_iota(jnp.int32, (tok, tok), 0)
    cols = lax.broadcasted_iota(jnp.int32, (tok, tok), 1)
    bias[0] = jnp.where(same_doc(0) & (rows >= cols), 0.0, NEG)

    def own_piece(h, carry):
        piece(0, h, 0, True)
        return carry

    lax.fori_loop(0, heads, own_piece, 0)

    turn = 3
    x_third = x * (7 - 4 * y) + (1 - x)
    y_third = x * (3 + 4 * y) + (1 - x) * 5

    def pick(place):
        z_slot = jnp.where(place < turn, 4, jnp.where(place < 2 * turn, 8, REACH))
        x_slot = jnp.where(place < turn, 3 - 2 * x, jnp.where(place < 2 * turn, 7 - 2 * x, x_third))
        y_slot = jnp.where(place < turn, 2, jnp.where(place < 2 * turn, 6, y_third))
        j = place % turn
        late = place >= 2 * turn
        first = jnp.where(late, x_slot, z_slot)
        second = jnp.where(late, y_slot, x_slot)
        third = jnp.where(late, z_slot, y_slot)
        return jnp.where(j == 0, first, jnp.where(j == 1, second, third))

    def arrive(t, carry):
        around = t // (turn * heads)
        inside = t % (turn * heads)
        h = inside // turn
        j = inside % turn
        s = pick(around * turn + j)

        @pl.when(me >= s)
        def _():
            pltpu.make_async_copy(kv.at[s, h], kv.at[s, h], recv_sem.at[s, h]).wait()

            @pl.when(h == 0)
            def _():
                pltpu.make_async_copy(docs.at[s], docs.at[s], drecv_sem.at[s]).wait()

            forward(s, h)

            @pl.when(h == 0)
            def _():
                bias[j] = jnp.where(same_doc(s), 0.0, NEG)

            piece(s, h, j, False)

        return carry

    lax.fori_loop(0, REACH * heads, arrive, 0)

    def finish(head, carry):
        total = jnp.sum(l_s[head], axis=1, keepdims=True)
        att[:, pl.ds(pl.multiple_of(head * HEAD_WIDTH, HEAD_WIDTH), HEAD_WIDTH)] = (
            acc[head] / total
        ).astype(jnp.bfloat16)
        return carry

    lax.fori_loop(0, heads * group, finish, 0)
    weight_copy.wait()

    half = out_ref.shape[0]
    tiles = out_ref.shape[1] // OUT_TILE
    keep = pl.multiple_of(core * half, half)
    give = pl.multiple_of((1 - core) * half, half)

    def swap_copy(i):
        return pltpu.make_async_remote_copy(
            src_ref=theirs.at[i],
            dst_ref=swapped.at[i],
            send_sem=osend_sem.at[i],
            recv_sem=orecv_sem.at[i],
            device_id={"head": 1 - core},
        )

    def project(i, carry):
        columns = pl.ds(pl.multiple_of(i * OUT_TILE, OUT_TILE), OUT_TILE)
        part[...] = jnp.dot(att[...], w_vm[:, columns], preferred_element_type=jnp.float32)
        theirs[i] = part[pl.ds(give, half), :].astype(jnp.bfloat16)
        swap_copy(i).start()
        out_ref[:, columns] = part[pl.ds(keep, half), :].astype(jnp.bfloat16)
        return carry

    lax.fori_loop(0, tiles, project, 0)

    def combine(i, carry):
        swap_copy(i).wait()
        columns = pl.ds(pl.multiple_of(i * OUT_TILE, OUT_TILE), OUT_TILE)
        out_ref[:, columns] = (
            out_ref[:, columns].astype(jnp.float32) + swapped[i].astype(jnp.float32)
        ).astype(jnp.bfloat16)
        return carry

    lax.fori_loop(0, tiles, combine, 0)

    def settle(s, carry):
        for link in range(3):
            @pl.when(sends(link, s) & (me >= s))
            def _():
                doc_copy(link, s).wait_send()
                for h in range(heads):
                    chunk_copy(link, s, h).wait_send()
        return carry

    lax.fori_loop(0, SLOTS, settle, 0)


def fused_device(queries, key_matrix, value_matrix, doc_ids, out_weight):
    tok, width = queries.shape
    heads = key_matrix.shape[1] // HEAD_WIDTH
    query_heads = width // HEAD_WIDTH
    out_width = out_weight.shape[1]
    half = tok // 2
    tiles = out_width // OUT_TILE
    query_docs = jnp.broadcast_to(doc_ids[:, None], (tok, HEAD_WIDTH))
    key_docs = jnp.broadcast_to(doc_ids[None, :], (8, tok))
    vmem = pl.BlockSpec(memory_space=pltpu.VMEM)
    f32, bf16 = jnp.float32, jnp.bfloat16
    return pl.pallas_call(
        fused_kernel,
        out_shape=jax.ShapeDtypeStruct((half, out_width), bf16),
        in_specs=[vmem] * 5 + [pl.BlockSpec(memory_space=pl.ANY)],
        out_specs=vmem,
        scratch_shapes=[
            pltpu.VMEM((SLOTS, heads, 2, tok, HEAD_WIDTH), bf16),
            pltpu.VMEM((SLOTS, 8, tok), jnp.int32),
            pltpu.VMEM((3, tok, tok), f32),
            pltpu.VMEM((query_heads, tok, HEAD_WIDTH), f32),
            pltpu.VMEM((query_heads, tok, HEAD_WIDTH), f32),
            pltpu.VMEM((query_heads, tok, HEAD_WIDTH), f32),
            pltpu.VMEM((tok, width), bf16),
            pltpu.VMEM(out_weight.shape, bf16),
            pltpu.VMEM((tok, OUT_TILE), f32),
            pltpu.VMEM((tiles, half, OUT_TILE), bf16),
            pltpu.VMEM((tiles, half, OUT_TILE), bf16),
            pltpu.SemaphoreType.DMA((3, SLOTS, heads)),
            pltpu.SemaphoreType.DMA((SLOTS, heads)),
            pltpu.SemaphoreType.DMA((3, SLOTS)),
            pltpu.SemaphoreType.DMA((SLOTS,)),
            pltpu.SemaphoreType.DMA,
            pltpu.SemaphoreType.DMA((tiles,)),
            pltpu.SemaphoreType.DMA((tiles,)),
        ],
        compiler_params=pltpu.CompilerParams(
            collective_id=0, has_side_effects=True, vmem_limit_bytes=58 * 1024 * 1024
        ),
    )(queries, key_matrix, value_matrix, query_docs, key_docs, out_weight)


def solution(mesh):
    placed = (P("ctx", "head"), P("ctx", "head"), P("ctx", "head"), P("ctx"), P("head", None))
    neighbours = mesh.shape["ctx"] == 4 * PLANE and mesh.shape["head"] == 2
    return jax.shard_map(
        fused_device if neighbours else gathered_attention,
        mesh=mesh,
        in_specs=placed,
        out_specs=P(("ctx", "head"), None),
        check_vma=False,
    )
```

```python
import functools
import jax
import jax.numpy as jnp
from jax import lax
from jax.experimental import pallas as pl
from jax.experimental.pallas import tpu as pltpu
from jax.sharding import PartitionSpec as P

HEAD_WIDTH = 128


def gathered_attention(queries, key_matrix, value_matrix, doc_ids, out_weight):
    tok_rows = queries.shape[0]
    kv_here = key_matrix.shape[1] // HEAD_WIDTH
    queries_per_group = queries.shape[1] // key_matrix.shape[1]
    all_rows = queries_per_group * tok_rows
    my_index = lax.axis_index("ctx")
    q_pos = my_index * tok_rows + jnp.arange(tok_rows, dtype=jnp.int32)
    q_rows = (
        queries.reshape(tok_rows, kv_here, queries_per_group, HEAD_WIDTH)
        .transpose(1, 2, 0, 3)
        .reshape(kv_here, all_rows, HEAD_WIDTH)
    )
    score_scale = HEAD_WIDTH ** (-0.5)
    running = jnp.full((kv_here, all_rows), -1e30, jnp.float32)
    part_keys = lax.all_gather(key_matrix, "ctx", axis=0, tiled=True)
    part_values = lax.all_gather(value_matrix, "ctx", axis=0, tiled=True)
    part_docs = lax.all_gather(doc_ids, "ctx", axis=0, tiled=True)
    key_count = part_keys.shape[0]
    k_pos = jnp.arange(key_count, dtype=jnp.int32)
    keys_three = part_keys.reshape(key_count, kv_here, HEAD_WIDTH).transpose(1, 0, 2)
    values_three = part_values.reshape(key_count, kv_here, HEAD_WIDTH).transpose(1, 0, 2)
    scores = (
        jnp.einsum("hqd,hkd->hqk", q_rows, keys_three, preferred_element_type=jnp.float32)
        * score_scale
    )
    allowed = (
        (doc_ids[:, None] == part_docs[None, :])
        & (q_pos[:, None] >= k_pos[None, :])
        & (k_pos[None, :] >= 0)
    )
    allowed = jnp.tile(allowed, (queries_per_group, 1))[None]
    scores = jnp.where(allowed, scores, jnp.float32(-1e30))
    new_max = jnp.maximum(running, jnp.max(scores, axis=-1))
    weights = jnp.where(allowed, jnp.exp(scores - new_max[..., None]), jnp.float32(0.0))
    denominator = jnp.sum(weights, axis=-1)
    weighted = jnp.einsum(
        "hqk,hkd->hqd",
        weights.astype(jnp.bfloat16),
        values_three,
        preferred_element_type=jnp.float32,
    )
    running_state = (new_max, denominator, weighted)
    running, denominator, weighted = running_state
    attended = (weighted / denominator[..., None]).astype(jnp.bfloat16)
    attended = (
        attended.reshape(kv_here, queries_per_group, tok_rows, HEAD_WIDTH)
        .transpose(2, 0, 1, 3)
        .reshape(tok_rows, kv_here * queries_per_group * HEAD_WIDTH)
    )
    return lax.psum_scatter(
        jnp.dot(attended, out_weight, preferred_element_type=jnp.float32).astype(jnp.bfloat16),
        "head",
        scatter_dimension=0,
        tiled=True,
    )


NEG = -1e30
LOG2E = 1.4426950408889634
PLANE = 4
REACH = 9
SLOTS = REACH + 1
OUT_TILE = 512


def fused_kernel(
    q_ref, k_ref, v_ref, doc_ref, w_hbm, out_ref,
    kv, docs, q_wide, k_wide, v_wide, m_s, acc, att, w_vm, part, theirs, swapped,
    send_sem, recv_sem, dsend_sem, drecv_sem, w_sem, osend_sem, orecv_sem,
):
    tok = q_ref.shape[0]
    heads = k_ref.shape[1] // HEAD_WIDTH
    group = q_ref.shape[1] // k_ref.shape[1]
    me = lax.axis_index("ctx")
    core = lax.axis_index("head")
    z, y, x = me // PLANE, (me // 2) % 2, me % 2
    dx, dy = 1 - 2 * x, 2 - 4 * y
    x_src = (4 * x, 4 + 4 * x, 2 + 4 * (1 - x) * (1 - y))
    y_src = (4 * y, 4 + 4 * y, 3 + 4 * y + x * (2 - 4 * y))
    z_src = (0, 4, 5)
    planes = lax.axis_size("ctx") // PLANE
    links = (
        (x_src, dx, None),
        (y_src, dy, None),
        (z_src, PLANE, z < planes - 1),
    )

    barrier = pltpu.get_barrier_semaphore()
    pl.semaphore_signal(barrier, inc=1, device_id={"ctx": me + dx})
    pl.semaphore_signal(barrier, inc=1, device_id={"ctx": me + dy})
    pl.semaphore_signal(barrier, inc=1, device_id={"head": 1 - core})

    @pl.when(z < planes - 1)
    def _():
        pl.semaphore_signal(barrier, inc=1, device_id={"ctx": me + PLANE})

    @pl.when(z > 0)
    def _():
        pl.semaphore_signal(barrier, inc=1, device_id={"ctx": me - PLANE})

    weight_copy = pltpu.make_async_copy(w_hbm, w_vm, w_sem)
    weight_copy.start()
    for h in range(heads):
        columns = pl.ds(h * HEAD_WIDTH, HEAD_WIDTH)
        kv[0, h, 0] = k_ref[:, columns]
        kv[0, h, 1] = v_ref[:, columns]
    docs[0] = jnp.broadcast_to(doc_ref[...], docs.shape[1:])

    def blank(s, carry):
        docs[s] = jnp.full(docs.shape[1:], -1, jnp.int32)
        kv[s] = jnp.zeros(kv.shape[1:], kv.dtype)
        return carry

    lax.fori_loop(jnp.minimum(me + 1, SLOTS), SLOTS, blank, 0)

    peers = 3 + jnp.where(z > 0, 1, 0) + jnp.where(z < planes - 1, 1, 0)
    pl.semaphore_wait(barrier, peers)

    def chunk_copy(link, s, h):
        step = links[link][1]
        return pltpu.make_async_remote_copy(
            src_ref=kv.at[s, h],
            dst_ref=kv.at[s + step, h],
            send_sem=send_sem.at[link, s, h],
            recv_sem=recv_sem.at[s + step, h],
            device_id={"ctx": me + step},
        )

    def doc_copy(link, s):
        step = links[link][1]
        return pltpu.make_async_remote_copy(
            src_ref=docs.at[s],
            dst_ref=docs.at[s + step],
            send_sem=dsend_sem.at[link, s],
            recv_sem=drecv_sem.at[s + step],
            device_id={"ctx": me + step},
        )

    def sends(link, s):
        sources, _, also = links[link]
        here = (s == sources[0]) | (s == sources[1]) | (s == sources[2])
        if also is not None:
            here = here & also
        return here

    def forward(s, h):
        for link in (2, 0, 1):
            @pl.when(sends(link, s))
            def _():
                @pl.when(h == 0)
                def _():
                    doc_copy(link, s).start()

                chunk_copy(link, s, h).start()

    def send_own(h, carry):
        forward(jnp.int32(0), h)
        return carry

    lax.fori_loop(0, heads, send_own, 0)

    score_scale = HEAD_WIDTH ** (-0.5) * LOG2E
    doc_rows = lax.broadcasted_iota(jnp.int32, (HEAD_WIDTH, tok), 0)

    def doc_columns(s, same, other):
        flags = jnp.where(docs[s, 0:1, :] == doc_rows, same, other).astype(jnp.float32)
        return flags.T.astype(jnp.bfloat16)

    own_docs = doc_columns(0, 1.0, 0.0)
    for head in range(heads * group):
        q_wide[head, :, :HEAD_WIDTH] = q_ref[:, head * HEAD_WIDTH:(head + 1) * HEAD_WIDTH]
        q_wide[head, :, HEAD_WIDTH:] = own_docs
    v_wide[:, HEAD_WIDTH:] = jnp.ones((v_wide.shape[0], HEAD_WIDTH), jnp.bfloat16)

    def fill(j, s, h):
        k_wide[j * tok:(j + 1) * tok, :HEAD_WIDTH] = kv[s, h, 0]
        v_wide[j * tok:(j + 1) * tok, :HEAD_WIDTH] = kv[s, h, 1]

        @pl.when(h == 0)
        def _():
            k_wide[j * tok:(j + 1) * tok, HEAD_WIDTH:] = doc_columns(s, 0.0, NEG)

    def piece(h, count, first):
        keys = k_wide[:count]
        values = v_wide[:count]

        def score(r):
            return lax.dot_general(
                q_wide[h * group + r], keys, (((1,), (1,)), ((), ())),
                preferred_element_type=jnp.float32,
            )

        upcoming = score(0)
        for r in range(group):
            scores = upcoming
            if r + 1 < group:
                upcoming = score(r + 1)
            head = h * group + r
            if first:
                rows = lax.broadcasted_iota(jnp.int32, (tok, tok), 0)
                cols = lax.broadcasted_iota(jnp.int32, (tok, tok), 1)
                scores = jnp.where(rows >= cols, scores, NEG)
            top = jnp.broadcast_to(
                jnp.max(scores, axis=1, keepdims=True), (tok, HEAD_WIDTH)
            )
            if not first:
                before = m_s[head]
                top = jnp.maximum(before, top)
            shift = jnp.concatenate([top * score_scale] * (count // HEAD_WIDTH), axis=1)
            weights = jnp.exp2(scores * score_scale - shift).astype(jnp.bfloat16)
            summed = jnp.dot(weights, values, preferred_element_type=jnp.float32)
            if not first:
                fade = jnp.exp2((before - top) * score_scale)
                summed = summed + acc[head] * jnp.concatenate([fade, fade], axis=1)
            m_s[head] = top
            acc[head] = summed

    def own_piece(h, carry):
        fill(0, 0, h)
        piece(h, tok, True)
        return carry

    lax.fori_loop(0, heads, own_piece, 0)

    turn = 3
    x_third = x * (7 - 4 * y) + (1 - x)
    y_third = x * (3 + 4 * y) + (1 - x) * 5

    def pick(place):
        z_slot = jnp.where(place < turn, 4, jnp.where(place < 2 * turn, 8, REACH))
        x_slot = jnp.where(place < turn, 3 - 2 * x, jnp.where(place < 2 * turn, 7 - 2 * x, x_third))
        y_slot = jnp.where(place < turn, 2, jnp.where(place < 2 * turn, 6, y_third))
        j = place % turn
        late = place >= 2 * turn
        first = jnp.where(late, x_slot, z_slot)
        second = jnp.where(late, y_slot, x_slot)
        third = jnp.where(late, z_slot, y_slot)
        return jnp.where(j == 0, first, jnp.where(j == 1, second, third))

    def arrive(t, carry):
        around = t // heads
        h = t % heads
        for j in range(turn):
            s = pick(around * turn + j)

            @pl.when(me >= s)
            def _():
                pltpu.make_async_copy(kv.at[s, h], kv.at[s, h], recv_sem.at[s, h]).wait()

                @pl.when(h == 0)
                def _():
                    pltpu.make_async_copy(docs.at[s], docs.at[s], drecv_sem.at[s]).wait()

                forward(s, h)

        for j in range(turn):
            fill(j, pick(around * turn + j), h)
        piece(h, turn * tok, False)
        return carry

    lax.fori_loop(0, REACH // turn * heads, arrive, 0)

    def finish(head, carry):
        att[:, pl.ds(pl.multiple_of(head * HEAD_WIDTH, HEAD_WIDTH), HEAD_WIDTH)] = (
            acc[head, :, :HEAD_WIDTH] / acc[head, :, HEAD_WIDTH:]
        ).astype(jnp.bfloat16)
        return carry

    lax.fori_loop(0, heads * group, finish, 0)
    weight_copy.wait()

    half = out_ref.shape[0]
    tiles = out_ref.shape[1] // OUT_TILE
    keep = pl.multiple_of(core * half, half)
    give = pl.multiple_of((1 - core) * half, half)

    def swap_copy(i):
        return pltpu.make_async_remote_copy(
            src_ref=theirs.at[i],
            dst_ref=swapped.at[i],
            send_sem=osend_sem.at[i],
            recv_sem=orecv_sem.at[i],
            device_id={"head": 1 - core},
        )

    def project(i, carry):
        columns = pl.ds(pl.multiple_of(i * OUT_TILE, OUT_TILE), OUT_TILE)
        part[...] = jnp.dot(att[...], w_vm[:, columns], preferred_element_type=jnp.float32)
        theirs[i] = part[pl.ds(give, half), :].astype(jnp.bfloat16)
        swap_copy(i).start()
        out_ref[:, columns] = part[pl.ds(keep, half), :].astype(jnp.bfloat16)
        return carry

    lax.fori_loop(0, tiles, project, 0)

    def combine(i, carry):
        swap_copy(i).wait()
        columns = pl.ds(pl.multiple_of(i * OUT_TILE, OUT_TILE), OUT_TILE)
        out_ref[:, columns] = (
            out_ref[:, columns].astype(jnp.float32) + swapped[i].astype(jnp.float32)
        ).astype(jnp.bfloat16)
        return carry

    lax.fori_loop(0, tiles, combine, 0)

    def settle(s, carry):
        for link in range(3):
            @pl.when(sends(link, s) & (me >= s))
            def _():
                doc_copy(link, s).wait_send()
                for h in range(heads):
                    chunk_copy(link, s, h).wait_send()
        return carry

    lax.fori_loop(0, SLOTS, settle, 0)


def fused_device(queries, key_matrix, value_matrix, doc_ids, out_weight):
    tok, width = queries.shape
    heads = key_matrix.shape[1] // HEAD_WIDTH
    query_heads = width // HEAD_WIDTH
    out_width = out_weight.shape[1]
    half = tok // 2
    tiles = out_width // OUT_TILE
    vmem = pl.BlockSpec(memory_space=pltpu.VMEM)
    f32, bf16 = jnp.float32, jnp.bfloat16
    return pl.pallas_call(
        fused_kernel,
        out_shape=jax.ShapeDtypeStruct((half, out_width), bf16),
        in_specs=[vmem] * 4 + [pl.BlockSpec(memory_space=pl.ANY)],
        out_specs=vmem,
        scratch_shapes=[
            pltpu.VMEM((SLOTS, heads, 2, tok, HEAD_WIDTH), bf16),
            pltpu.VMEM((SLOTS, 8, tok), jnp.int32),
            pltpu.VMEM((query_heads, tok, 2 * HEAD_WIDTH), bf16),
            pltpu.VMEM((3 * tok, 2 * HEAD_WIDTH), bf16),
            pltpu.VMEM((3 * tok, 2 * HEAD_WIDTH), bf16),
            pltpu.VMEM((query_heads, tok, HEAD_WIDTH), f32),
            pltpu.VMEM((query_heads, tok, 2 * HEAD_WIDTH), f32),
            pltpu.VMEM((tok, width), bf16),
            pltpu.VMEM(out_weight.shape, bf16),
            pltpu.VMEM((tok, OUT_TILE), f32),
            pltpu.VMEM((tiles, half, OUT_TILE), bf16),
            pltpu.VMEM((tiles, half, OUT_TILE), bf16),
            pltpu.SemaphoreType.DMA((3, SLOTS, heads)),
            pltpu.SemaphoreType.DMA((SLOTS, heads)),
            pltpu.SemaphoreType.DMA((3, SLOTS)),
            pltpu.SemaphoreType.DMA((SLOTS,)),
            pltpu.SemaphoreType.DMA,
            pltpu.SemaphoreType.DMA((tiles,)),
            pltpu.SemaphoreType.DMA((tiles,)),
        ],
        compiler_params=pltpu.CompilerParams(
            collective_id=0, has_side_effects=True, vmem_limit_bytes=58 * 1024 * 1024
        ),
    )(queries, key_matrix, value_matrix, doc_ids[None, :], out_weight)


def solution(mesh):
    placed = (P("ctx", "head"), P("ctx", "head"), P("ctx", "head"), P("ctx"), P("head", None))
    neighbours = mesh.shape["ctx"] == 4 * PLANE and mesh.shape["head"] == 2
    return jax.shard_map(
        fused_device if neighbours else gathered_attention,
        mesh=mesh,
        in_specs=placed,
        out_specs=P(("ctx", "head"), None),
        check_vma=False,
    )
```

```python
import functools
import jax
import jax.numpy as jnp
from jax import lax
from jax.experimental import pallas as pl
from jax.experimental.pallas import tpu as pltpu
from jax.sharding import PartitionSpec as P

HEAD_WIDTH = 128


def gathered_attention(queries, key_matrix, value_matrix, doc_ids, out_weight):
    tok_rows = queries.shape[0]
    kv_here = key_matrix.shape[1] // HEAD_WIDTH
    queries_per_group = queries.shape[1] // key_matrix.shape[1]
    all_rows = queries_per_group * tok_rows
    my_index = lax.axis_index("ctx")
    q_pos = my_index * tok_rows + jnp.arange(tok_rows, dtype=jnp.int32)
    q_rows = (
        queries.reshape(tok_rows, kv_here, queries_per_group, HEAD_WIDTH)
        .transpose(1, 2, 0, 3)
        .reshape(kv_here, all_rows, HEAD_WIDTH)
    )
    score_scale = HEAD_WIDTH ** (-0.5)
    running = jnp.full((kv_here, all_rows), -1e30, jnp.float32)
    part_keys = lax.all_gather(key_matrix, "ctx", axis=0, tiled=True)
    part_values = lax.all_gather(value_matrix, "ctx", axis=0, tiled=True)
    part_docs = lax.all_gather(doc_ids, "ctx", axis=0, tiled=True)
    key_count = part_keys.shape[0]
    k_pos = jnp.arange(key_count, dtype=jnp.int32)
    keys_three = part_keys.reshape(key_count, kv_here, HEAD_WIDTH).transpose(1, 0, 2)
    values_three = part_values.reshape(key_count, kv_here, HEAD_WIDTH).transpose(1, 0, 2)
    scores = (
        jnp.einsum("hqd,hkd->hqk", q_rows, keys_three, preferred_element_type=jnp.float32)
        * score_scale
    )
    allowed = (
        (doc_ids[:, None] == part_docs[None, :])
        & (q_pos[:, None] >= k_pos[None, :])
        & (k_pos[None, :] >= 0)
    )
    allowed = jnp.tile(allowed, (queries_per_group, 1))[None]
    scores = jnp.where(allowed, scores, jnp.float32(-1e30))
    new_max = jnp.maximum(running, jnp.max(scores, axis=-1))
    weights = jnp.where(allowed, jnp.exp(scores - new_max[..., None]), jnp.float32(0.0))
    denominator = jnp.sum(weights, axis=-1)
    weighted = jnp.einsum(
        "hqk,hkd->hqd",
        weights.astype(jnp.bfloat16),
        values_three,
        preferred_element_type=jnp.float32,
    )
    running_state = (new_max, denominator, weighted)
    running, denominator, weighted = running_state
    attended = (weighted / denominator[..., None]).astype(jnp.bfloat16)
    attended = (
        attended.reshape(kv_here, queries_per_group, tok_rows, HEAD_WIDTH)
        .transpose(2, 0, 1, 3)
        .reshape(tok_rows, kv_here * queries_per_group * HEAD_WIDTH)
    )
    return lax.psum_scatter(
        jnp.dot(attended, out_weight, preferred_element_type=jnp.float32).astype(jnp.bfloat16),
        "head",
        scatter_dimension=0,
        tiled=True,
    )


NEG = -1e30
LOG2E = 1.4426950408889634
PLANE = 4
REACH = 9
SLOTS = REACH + 1
OUT_TILE = 512


def fused_kernel(
    q_ref, k_ref, v_ref, doc_ref, w_hbm, out_ref,
    kv, docs, flags, q_wide, k_wide, v_wide, m_s, acc, att, w_vm, total, theirs, swapped,
    send_sem, recv_sem, dsend_sem, drecv_sem, w_sem, osend_sem, orecv_sem,
):
    tok = q_ref.shape[0]
    heads = k_ref.shape[1] // HEAD_WIDTH
    group = q_ref.shape[1] // k_ref.shape[1]
    me = lax.axis_index("ctx")
    core = lax.axis_index("head")
    z, y, x = me // PLANE, (me // 2) % 2, me % 2
    dx, dy = 1 - 2 * x, 2 - 4 * y
    x_src = (4 * x, 4 + 4 * x, 2 + 4 * (1 - x) * (1 - y))
    y_src = (4 * y, 4 + 4 * y, 3 + 4 * y + x * (2 - 4 * y))
    z_src = (0, 4, 5)
    planes = lax.axis_size("ctx") // PLANE
    links = (
        (x_src, dx, None),
        (y_src, dy, None),
        (z_src, PLANE, z < planes - 1),
    )

    barrier = pltpu.get_barrier_semaphore()
    pl.semaphore_signal(barrier, inc=1, device_id={"ctx": me + dx})
    pl.semaphore_signal(barrier, inc=1, device_id={"ctx": me + dy})
    pl.semaphore_signal(barrier, inc=1, device_id={"head": 1 - core})

    @pl.when(z < planes - 1)
    def _():
        pl.semaphore_signal(barrier, inc=1, device_id={"ctx": me + PLANE})

    @pl.when(z > 0)
    def _():
        pl.semaphore_signal(barrier, inc=1, device_id={"ctx": me - PLANE})

    weight_copy = pltpu.make_async_copy(w_hbm, w_vm, w_sem)
    weight_copy.start()
    for h in range(heads):
        columns = pl.ds(h * HEAD_WIDTH, HEAD_WIDTH)
        kv[0, h, 0] = k_ref[:, columns]
        kv[0, h, 1] = v_ref[:, columns]
    docs[0] = jnp.broadcast_to(doc_ref[...], docs.shape[1:])

    def blank(s, carry):
        docs[s] = jnp.full(docs.shape[1:], -1, jnp.int32)
        kv[s] = jnp.zeros(kv.shape[1:], kv.dtype)
        return carry

    lax.fori_loop(jnp.minimum(me + 1, SLOTS), SLOTS, blank, 0)

    peers = 3 + jnp.where(z > 0, 1, 0) + jnp.where(z < planes - 1, 1, 0)
    pl.semaphore_wait(barrier, peers)

    def chunk_copy(link, s, h):
        step = links[link][1]
        return pltpu.make_async_remote_copy(
            src_ref=kv.at[s, h],
            dst_ref=kv.at[s + step, h],
            send_sem=send_sem.at[link, s, h],
            recv_sem=recv_sem.at[s + step, h],
            device_id={"ctx": me + step},
        )

    def doc_copy(link, s):
        step = links[link][1]
        return pltpu.make_async_remote_copy(
            src_ref=docs.at[s],
            dst_ref=docs.at[s + step],
            send_sem=dsend_sem.at[link, s],
            recv_sem=drecv_sem.at[s + step],
            device_id={"ctx": me + step},
        )

    def sends(link, s):
        sources, _, also = links[link]
        here = (s == sources[0]) | (s == sources[1]) | (s == sources[2])
        if also is not None:
            here = here & also
        return here

    def forward(s, h):
        for link in (2, 0, 1):
            @pl.when(sends(link, s))
            def _():
                @pl.when(h == 0)
                def _():
                    doc_copy(link, s).start()

                chunk_copy(link, s, h).start()

    def send_own(h, carry):
        forward(jnp.int32(0), h)
        return carry

    lax.fori_loop(0, 2, send_own, 0)

    score_scale = HEAD_WIDTH ** (-0.5) * LOG2E
    doc_rows = lax.broadcasted_iota(jnp.int32, (HEAD_WIDTH, tok), 0)

    def doc_columns(s, same, other):
        flags = jnp.where(docs[s, 0:1, :] == doc_rows, same, other).astype(jnp.float32)
        return flags.T.astype(jnp.bfloat16)

    own_docs = doc_columns(0, 1.0, 0.0)
    for r in range(group):
        q_wide[r, :, HEAD_WIDTH:] = own_docs
    v_wide[:, HEAD_WIDTH:] = jnp.ones((v_wide.shape[0], HEAD_WIDTH), jnp.bfloat16)

    def fill(j, s, h):
        @pl.when(h == 0)
        def _():
            flags[s] = doc_columns(s, 0.0, NEG)

        k_wide[j * tok:(j + 1) * tok, :HEAD_WIDTH] = kv[s, h, 0]
        k_wide[j * tok:(j + 1) * tok, HEAD_WIDTH:] = flags[s]
        v_wide[j * tok:(j + 1) * tok, :HEAD_WIDTH] = kv[s, h, 1]

    def piece(count, first):
        keys = k_wide[:count]
        values = v_wide[:count]

        def score(r):
            return lax.dot_general(
                q_wide[r], keys, (((1,), (1,)), ((), ())),
                preferred_element_type=jnp.float32,
            )

        upcoming = score(0)
        for r in range(group):
            scores = upcoming
            if r + 1 < group:
                upcoming = score(r + 1)
            if first:
                rows = lax.broadcasted_iota(jnp.int32, (tok, tok), 0)
                cols = lax.broadcasted_iota(jnp.int32, (tok, tok), 1)
                scores = jnp.where(rows >= cols, scores, NEG)
            top = jnp.broadcast_to(
                jnp.max(scores, axis=1, keepdims=True), (tok, HEAD_WIDTH)
            )
            if not first:
                before = m_s[r]
                top = jnp.maximum(before, top)
            shift = jnp.concatenate([top * score_scale] * (count // HEAD_WIDTH), axis=1)
            weights = jnp.exp2(scores * score_scale - shift).astype(jnp.bfloat16)
            summed = jnp.dot(weights, values, preferred_element_type=jnp.float32)
            if not first:
                fade = jnp.exp2((before - top) * score_scale)
                summed = summed + acc[r] * jnp.concatenate([fade, fade], axis=1)
            m_s[r] = top
            acc[r] = summed

    turn = 3
    x_third = x * (7 - 4 * y) + (1 - x)
    y_third = x * (3 + 4 * y) + (1 - x) * 5

    def pick(place):
        z_slot = jnp.where(place < turn, 4, jnp.where(place < 2 * turn, 8, REACH))
        x_slot = jnp.where(place < turn, 3 - 2 * x, jnp.where(place < 2 * turn, 7 - 2 * x, x_third))
        y_slot = jnp.where(place < turn, 2, jnp.where(place < 2 * turn, 6, y_third))
        j = place % turn
        late = place >= 2 * turn
        first = jnp.where(late, x_slot, z_slot)
        second = jnp.where(late, y_slot, x_slot)
        third = jnp.where(late, z_slot, y_slot)
        return jnp.where(j == 0, first, jnp.where(j == 1, second, third))

    half = out_ref.shape[0]
    tiles = out_ref.shape[1] // OUT_TILE
    keep = pl.multiple_of(core * half, half)
    give = pl.multiple_of((1 - core) * half, half)
    span = group * HEAD_WIDTH

    def tile_columns(i):
        return pl.ds(pl.multiple_of(i * OUT_TILE, OUT_TILE), OUT_TILE)

    def swap_copy(i):
        return pltpu.make_async_remote_copy(
            src_ref=theirs.at[i],
            dst_ref=swapped.at[i],
            send_sem=osend_sem.at[i],
            recv_sem=orecv_sem.at[i],
            device_id={"head": 1 - core},
        )

    def one_head(h, carry):
        @pl.when((h >= 1) & (h < heads - 1))
        def _():
            forward(jnp.int32(0), h + 1)

        for r in range(group):
            place = pl.multiple_of(h * span + r * HEAD_WIDTH, HEAD_WIDTH)
            q_wide[r, :, :HEAD_WIDTH] = q_ref[:, pl.ds(place, HEAD_WIDTH)]
        fill(0, 0, h)
        piece(tok, True)

        def arrive(around, inner):
            for j in range(turn):
                s = pick(around * turn + j)

                @pl.when(me >= s)
                def _():
                    pltpu.make_async_copy(kv.at[s, h], kv.at[s, h], recv_sem.at[s, h]).wait()

                    @pl.when(h == 0)
                    def _():
                        pltpu.make_async_copy(docs.at[s], docs.at[s], drecv_sem.at[s]).wait()

                    forward(s, h)

            for j in range(turn):
                fill(j, pick(around * turn + j), h)
            piece(turn * tok, False)
            return inner

        lax.fori_loop(0, REACH // turn, arrive, 0)

        for r in range(group):
            att[:, r * HEAD_WIDTH:(r + 1) * HEAD_WIDTH] = (
                acc[r, :, :HEAD_WIDTH] / acc[r, :, HEAD_WIDTH:]
            ).astype(jnp.bfloat16)

        @pl.when(h == 0)
        def _():
            weight_copy.wait()

        weight_rows = pl.ds(pl.multiple_of(h * span, span), span)

        def project(i, inner):
            columns = tile_columns(i)
            share = jnp.dot(
                att[...], w_vm[weight_rows, columns], preferred_element_type=jnp.float32
            )

            @pl.when(h == 0)
            def _():
                total[:, columns] = share

            @pl.when(h > 0)
            def _():
                total[:, columns] += share

            @pl.when(h == heads - 1)
            def _():
                theirs[i] = total[pl.ds(give, half), columns].astype(jnp.bfloat16)
                swap_copy(i).start()

            return inner

        lax.fori_loop(0, tiles, project, 0)
        return carry

    lax.fori_loop(0, heads, one_head, 0)

    def combine(i, carry):
        swap_copy(i).wait()
        columns = tile_columns(i)
        out_ref[:, columns] = (
            total[pl.ds(keep, half), columns] + swapped[i].astype(jnp.float32)
        ).astype(jnp.bfloat16)
        return carry

    lax.fori_loop(0, tiles, combine, 0)

    def settle(s, carry):
        for link in range(3):
            @pl.when(sends(link, s) & (me >= s))
            def _():
                doc_copy(link, s).wait_send()
                for h in range(heads):
                    chunk_copy(link, s, h).wait_send()
        return carry

    lax.fori_loop(0, SLOTS, settle, 0)


def fused_device(queries, key_matrix, value_matrix, doc_ids, out_weight):
    tok, width = queries.shape
    heads = key_matrix.shape[1] // HEAD_WIDTH
    group = width // key_matrix.shape[1]
    out_width = out_weight.shape[1]
    half = tok // 2
    tiles = out_width // OUT_TILE
    vmem = pl.BlockSpec(memory_space=pltpu.VMEM)
    f32, bf16 = jnp.float32, jnp.bfloat16
    return pl.pallas_call(
        fused_kernel,
        out_shape=jax.ShapeDtypeStruct((half, out_width), bf16),
        in_specs=[vmem] * 4 + [pl.BlockSpec(memory_space=pl.ANY)],
        out_specs=vmem,
        scratch_shapes=[
            pltpu.VMEM((SLOTS, heads, 2, tok, HEAD_WIDTH), bf16),
            pltpu.VMEM((SLOTS, 8, tok), jnp.int32),
            pltpu.VMEM((SLOTS, tok, HEAD_WIDTH), bf16),
            pltpu.VMEM((group, tok, 2 * HEAD_WIDTH), bf16),
            pltpu.VMEM((3 * tok, 2 * HEAD_WIDTH), bf16),
            pltpu.VMEM((3 * tok, 2 * HEAD_WIDTH), bf16),
            pltpu.VMEM((group, tok, HEAD_WIDTH), f32),
            pltpu.VMEM((group, tok, 2 * HEAD_WIDTH), f32),
            pltpu.VMEM((tok, group * HEAD_WIDTH), bf16),
            pltpu.VMEM(out_weight.shape, bf16),
            pltpu.VMEM((tok, out_width), f32),
            pltpu.VMEM((tiles, half, OUT_TILE), bf16),
            pltpu.VMEM((tiles, half, OUT_TILE), bf16),
            pltpu.SemaphoreType.DMA((3, SLOTS, heads)),
            pltpu.SemaphoreType.DMA((SLOTS, heads)),
            pltpu.SemaphoreType.DMA((3, SLOTS)),
            pltpu.SemaphoreType.DMA((SLOTS,)),
            pltpu.SemaphoreType.DMA,
            pltpu.SemaphoreType.DMA((tiles,)),
            pltpu.SemaphoreType.DMA((tiles,)),
        ],
        compiler_params=pltpu.CompilerParams(
            collective_id=0, has_side_effects=True, vmem_limit_bytes=58 * 1024 * 1024
        ),
    )(queries, key_matrix, value_matrix, doc_ids.reshape(1, tok), out_weight)


def solution(mesh):
    placed = (P("ctx", "head"), P("ctx", "head"), P("ctx", "head"), P("ctx"), P("head", None))
    neighbours = mesh.shape["ctx"] == 4 * PLANE and mesh.shape["head"] == 2
    return jax.shard_map(
        fused_device if neighbours else gathered_attention,
        mesh=mesh,
        in_specs=placed,
        out_specs=P(("ctx", "head"), None),
        check_vma=False,
    )
```

```python
import functools
import jax
import jax.numpy as jnp
from jax import lax
from jax.experimental import pallas as pl
from jax.experimental.pallas import tpu as pltpu
from jax.sharding import PartitionSpec as P

HEAD_WIDTH = 128


def gathered_attention(queries, key_matrix, value_matrix, doc_ids, out_weight):
    tok_rows = queries.shape[0]
    kv_here = key_matrix.shape[1] // HEAD_WIDTH
    queries_per_group = queries.shape[1] // key_matrix.shape[1]
    all_rows = queries_per_group * tok_rows
    my_index = lax.axis_index("ctx")
    q_pos = my_index * tok_rows + jnp.arange(tok_rows, dtype=jnp.int32)
    q_rows = (
        queries.reshape(tok_rows, kv_here, queries_per_group, HEAD_WIDTH)
        .transpose(1, 2, 0, 3)
        .reshape(kv_here, all_rows, HEAD_WIDTH)
    )
    score_scale = HEAD_WIDTH ** (-0.5)
    running = jnp.full((kv_here, all_rows), -1e30, jnp.float32)
    part_keys = lax.all_gather(key_matrix, "ctx", axis=0, tiled=True)
    part_values = lax.all_gather(value_matrix, "ctx", axis=0, tiled=True)
    part_docs = lax.all_gather(doc_ids, "ctx", axis=0, tiled=True)
    key_count = part_keys.shape[0]
    k_pos = jnp.arange(key_count, dtype=jnp.int32)
    keys_three = part_keys.reshape(key_count, kv_here, HEAD_WIDTH).transpose(1, 0, 2)
    values_three = part_values.reshape(key_count, kv_here, HEAD_WIDTH).transpose(1, 0, 2)
    scores = (
        jnp.einsum("hqd,hkd->hqk", q_rows, keys_three, preferred_element_type=jnp.float32)
        * score_scale
    )
    allowed = (
        (doc_ids[:, None] == part_docs[None, :])
        & (q_pos[:, None] >= k_pos[None, :])
        & (k_pos[None, :] >= 0)
    )
    allowed = jnp.tile(allowed, (queries_per_group, 1))[None]
    scores = jnp.where(allowed, scores, jnp.float32(-1e30))
    new_max = jnp.maximum(running, jnp.max(scores, axis=-1))
    weights = jnp.where(allowed, jnp.exp(scores - new_max[..., None]), jnp.float32(0.0))
    denominator = jnp.sum(weights, axis=-1)
    weighted = jnp.einsum(
        "hqk,hkd->hqd",
        weights.astype(jnp.bfloat16),
        values_three,
        preferred_element_type=jnp.float32,
    )
    running_state = (new_max, denominator, weighted)
    running, denominator, weighted = running_state
    attended = (weighted / denominator[..., None]).astype(jnp.bfloat16)
    attended = (
        attended.reshape(kv_here, queries_per_group, tok_rows, HEAD_WIDTH)
        .transpose(2, 0, 1, 3)
        .reshape(tok_rows, kv_here * queries_per_group * HEAD_WIDTH)
    )
    return lax.psum_scatter(
        jnp.dot(attended, out_weight, preferred_element_type=jnp.float32).astype(jnp.bfloat16),
        "head",
        scatter_dimension=0,
        tiled=True,
    )


NEG = -1e30
LOG2E = 1.4426950408889634
PLANE = 4
REACH = 9
SLOTS = REACH + 1
OUT_TILE = 512


def fused_kernel(
    q_ref, k_ref, v_ref, doc_ref, w_hbm, out_ref,
    kv, docs, flags, q_wide, k_wide, v_wide, m_s, acc, att, w_vm, total, theirs, swapped,
    send_sem, recv_sem, dsend_sem, drecv_sem, w_sem, osend_sem, orecv_sem,
):
    tok = q_ref.shape[0]
    heads = k_ref.shape[1] // HEAD_WIDTH
    group = q_ref.shape[1] // k_ref.shape[1]
    me = lax.axis_index("ctx")
    core = lax.axis_index("head")
    z, y, x = me // PLANE, (me // 2) % 2, me % 2
    dx, dy = 1 - 2 * x, 2 - 4 * y
    x_src = (4 * x, 4 + 4 * x, 2 + 4 * (1 - x) * (1 - y))
    y_src = (4 * y, 4 + 4 * y, 3 + 4 * y + x * (2 - 4 * y))
    z_src = (0, 4, 5)
    planes = lax.axis_size("ctx") // PLANE
    links = (
        (x_src, dx, None),
        (y_src, dy, None),
        (z_src, PLANE, z < planes - 1),
    )

    barrier = pltpu.get_barrier_semaphore()
    pl.semaphore_signal(barrier, inc=1, device_id={"ctx": me + dx})
    pl.semaphore_signal(barrier, inc=1, device_id={"ctx": me + dy})
    pl.semaphore_signal(barrier, inc=1, device_id={"head": 1 - core})

    @pl.when(z < planes - 1)
    def _():
        pl.semaphore_signal(barrier, inc=1, device_id={"ctx": me + PLANE})

    @pl.when(z > 0)
    def _():
        pl.semaphore_signal(barrier, inc=1, device_id={"ctx": me - PLANE})

    weight_copy = pltpu.make_async_copy(w_hbm, w_vm, w_sem)
    weight_copy.start()
    for h in range(heads):
        columns = pl.ds(h * HEAD_WIDTH, HEAD_WIDTH)
        kv[0, h, 0] = k_ref[:, columns]
        kv[0, h, 1] = v_ref[:, columns]
    docs[0] = jnp.broadcast_to(doc_ref[...], docs.shape[1:])

    def blank(s, carry):
        docs[s] = jnp.full(docs.shape[1:], -1, jnp.int32)
        kv[s] = jnp.zeros(kv.shape[1:], kv.dtype)
        return carry

    lax.fori_loop(jnp.minimum(me + 1, SLOTS), SLOTS, blank, 0)

    peers = 3 + jnp.where(z > 0, 1, 0) + jnp.where(z < planes - 1, 1, 0)
    pl.semaphore_wait(barrier, peers)

    def chunk_copy(link, s, h):
        step = links[link][1]
        return pltpu.make_async_remote_copy(
            src_ref=kv.at[s, h],
            dst_ref=kv.at[s + step, h],
            send_sem=send_sem.at[link, s, h],
            recv_sem=recv_sem.at[s + step, h],
            device_id={"ctx": me + step},
        )

    def doc_copy(link, s):
        step = links[link][1]
        return pltpu.make_async_remote_copy(
            src_ref=docs.at[s],
            dst_ref=docs.at[s + step],
            send_sem=dsend_sem.at[link, s],
            recv_sem=drecv_sem.at[s + step],
            device_id={"ctx": me + step},
        )

    def sends(link, s, count=3):
        sources, _, also = links[link]
        here = s == sources[0]
        for i in range(1, count):
            here = here | (s == sources[i])
        if also is not None:
            here = here & also
        return here

    def start_send(link, s, h):
        @pl.when(h == 0)
        def _():
            doc_copy(link, s).start()

        chunk_copy(link, s, h).start()

    def forward(s, h):
        for link, count in ((2, 3), (0, 2), (1, 2)):
            @pl.when(sends(link, s, count))
            def _():
                start_send(link, s, h)

    def forward_last(h):
        for link in (0, 1):
            s = links[link][0][2]

            @pl.when(me >= s)
            def _():
                start_send(link, s, h)

    def send_own(h, carry):
        forward(jnp.int32(0), h)
        return carry

    lax.fori_loop(0, heads, send_own, 0)

    score_scale = HEAD_WIDTH ** (-0.5) * LOG2E
    doc_rows = lax.broadcasted_iota(jnp.int32, (HEAD_WIDTH, tok), 0)

    def doc_columns(s, same, other):
        flags = jnp.where(docs[s, 0:1, :] == doc_rows, same, other).astype(jnp.float32)
        return flags.T.astype(jnp.bfloat16)

    own_docs = doc_columns(0, 1.0, 0.0)
    for r in range(group):
        q_wide[r, :, HEAD_WIDTH:] = own_docs
    v_wide[:, HEAD_WIDTH:] = jnp.ones((v_wide.shape[0], HEAD_WIDTH), jnp.bfloat16)

    def fill(j, s, h):
        @pl.when(h == 0)
        def _():
            flags[s] = doc_columns(s, 0.0, NEG)

        k_wide[j * tok:(j + 1) * tok, :HEAD_WIDTH] = kv[s, h, 0]
        k_wide[j * tok:(j + 1) * tok, HEAD_WIDTH:] = flags[s]
        v_wide[j * tok:(j + 1) * tok, :HEAD_WIDTH] = kv[s, h, 1]

    def piece(h, count, first):
        for r in range(group):
            place = pl.multiple_of((h * group + r) * HEAD_WIDTH, HEAD_WIDTH)
            q_wide[r, :, :HEAD_WIDTH] = q_ref[:, pl.ds(place, HEAD_WIDTH)]
        keys = k_wide[:count]
        values = v_wide[:count]

        def score(r):
            return lax.dot_general(
                q_wide[r], keys, (((1,), (1,)), ((), ())),
                preferred_element_type=jnp.float32,
            )

        upcoming = score(0)
        for r in range(group):
            scores = upcoming
            head = h * group + r
            if r + 1 < group:
                upcoming = score(r + 1)
            if first:
                rows = lax.broadcasted_iota(jnp.int32, (tok, tok), 0)
                cols = lax.broadcasted_iota(jnp.int32, (tok, tok), 1)
                scores = jnp.where(rows >= cols, scores, NEG)
            top = jnp.broadcast_to(
                jnp.max(scores, axis=1, keepdims=True), (tok, HEAD_WIDTH)
            )
            if not first:
                before = m_s[head]
                top = jnp.maximum(before, top)
            shift = jnp.concatenate([top * score_scale] * (count // HEAD_WIDTH), axis=1)
            weights = jnp.exp2(scores * score_scale - shift).astype(jnp.bfloat16)
            summed = jnp.dot(weights, values, preferred_element_type=jnp.float32)
            if not first:
                fade = jnp.exp2((before - top) * score_scale)
                summed = summed + acc[head] * jnp.concatenate([fade, fade], axis=1)
            m_s[head] = top
            acc[head] = summed

    turn = 3
    x_third = x * (7 - 4 * y) + (1 - x)
    y_third = x * (3 + 4 * y) + (1 - x) * 5

    def pick(place):
        z_slot = jnp.where(place < turn, 4, jnp.where(place < 2 * turn, 8, REACH))
        x_slot = jnp.where(place < turn, 3 - 2 * x, jnp.where(place < 2 * turn, 7 - 2 * x, x_third))
        y_slot = jnp.where(place < turn, 2, jnp.where(place < 2 * turn, 6, y_third))
        j = place % turn
        late = place >= 2 * turn
        first = jnp.where(late, x_slot, z_slot)
        second = jnp.where(late, y_slot, x_slot)
        third = jnp.where(late, z_slot, y_slot)
        return jnp.where(j == 0, first, jnp.where(j == 1, second, third))

    half = out_ref.shape[0]
    tiles = out_ref.shape[1] // OUT_TILE
    keep = pl.multiple_of(core * half, half)
    give = pl.multiple_of((1 - core) * half, half)
    span = group * HEAD_WIDTH

    def tile_columns(i):
        return pl.ds(pl.multiple_of(i * OUT_TILE, OUT_TILE), OUT_TILE)

    def swap_copy(i):
        return pltpu.make_async_remote_copy(
            src_ref=theirs.at[i],
            dst_ref=swapped.at[i],
            send_sem=osend_sem.at[i],
            recv_sem=orecv_sem.at[i],
            device_id={"head": 1 - core},
        )

    def project_head(h):
        for r in range(group):
            head = h * group + r
            att[:, r * HEAD_WIDTH:(r + 1) * HEAD_WIDTH] = (
                acc[head, :, :HEAD_WIDTH] / acc[head, :, HEAD_WIDTH:]
            ).astype(jnp.bfloat16)

        @pl.when(h == 0)
        def _():
            weight_copy.wait()

        weight_rows = pl.ds(pl.multiple_of(h * span, span), span)

        def project(i, inner):
            columns = tile_columns(i)
            share = jnp.dot(
                att[...], w_vm[weight_rows, columns], preferred_element_type=jnp.float32
            )

            @pl.when(h == 0)
            def _():
                total[:, columns] = share

            @pl.when(h > 0)
            def _():
                total[:, columns] += share

            @pl.when(h == heads - 1)
            def _():
                theirs[i] = total[pl.ds(give, half), columns].astype(jnp.bfloat16)
                swap_copy(i).start()

            return inner

        lax.fori_loop(0, tiles, project, 0)

    def own_piece(h, carry):
        fill(0, 0, h)
        piece(h, tok, True)
        return carry

    lax.fori_loop(0, heads, own_piece, 0)
    lag = heads + 2

    def arrive(t, carry):
        around = t // heads
        h = t % heads

        @pl.when((t >= lag) & (t < lag + heads))
        def _():
            forward_last(t - lag)

        for j in range(turn):
            s = pick(around * turn + j)

            @pl.when(me >= s)
            def _():
                pltpu.make_async_copy(kv.at[s, h], kv.at[s, h], recv_sem.at[s, h]).wait()

                @pl.when(h == 0)
                def _():
                    pltpu.make_async_copy(docs.at[s], docs.at[s], drecv_sem.at[s]).wait()

                forward(s, h)

        for j in range(turn):
            fill(j, pick(around * turn + j), h)
        piece(h, turn * tok, False)

        @pl.when(around == REACH // turn - 1)
        def _():
            project_head(h)

        return carry

    lax.fori_loop(0, REACH // turn * heads, arrive, 0)

    def combine(i, carry):
        swap_copy(i).wait()
        columns = tile_columns(i)
        out_ref[:, columns] = (
            total[pl.ds(keep, half), columns] + swapped[i].astype(jnp.float32)
        ).astype(jnp.bfloat16)
        return carry

    lax.fori_loop(0, tiles, combine, 0)

    def settle(s, carry):
        for link in range(3):
            @pl.when(sends(link, s) & (me >= s))
            def _():
                doc_copy(link, s).wait_send()
                for h in range(heads):
                    chunk_copy(link, s, h).wait_send()
        return carry

    lax.fori_loop(0, SLOTS, settle, 0)


def fused_device(queries, key_matrix, value_matrix, doc_ids, out_weight):
    tok, width = queries.shape
    heads = key_matrix.shape[1] // HEAD_WIDTH
    group = width // key_matrix.shape[1]
    out_width = out_weight.shape[1]
    half = tok // 2
    tiles = out_width // OUT_TILE
    vmem = pl.BlockSpec(memory_space=pltpu.VMEM)
    f32, bf16 = jnp.float32, jnp.bfloat16
    return pl.pallas_call(
        fused_kernel,
        out_shape=jax.ShapeDtypeStruct((half, out_width), bf16),
        in_specs=[vmem] * 4 + [pl.BlockSpec(memory_space=pl.ANY)],
        out_specs=vmem,
        scratch_shapes=[
            pltpu.VMEM((SLOTS, heads, 2, tok, HEAD_WIDTH), bf16),
            pltpu.VMEM((SLOTS, 8, tok), jnp.int32),
            pltpu.VMEM((SLOTS, tok, HEAD_WIDTH), bf16),
            pltpu.VMEM((group, tok, 2 * HEAD_WIDTH), bf16),
            pltpu.VMEM((3 * tok, 2 * HEAD_WIDTH), bf16),
            pltpu.VMEM((3 * tok, 2 * HEAD_WIDTH), bf16),
            pltpu.VMEM((heads * group, tok, HEAD_WIDTH), f32),
            pltpu.VMEM((heads * group, tok, 2 * HEAD_WIDTH), f32),
            pltpu.VMEM((tok, group * HEAD_WIDTH), bf16),
            pltpu.VMEM(out_weight.shape, bf16),
            pltpu.VMEM((tok, out_width), f32),
            pltpu.VMEM((tiles, half, OUT_TILE), bf16),
            pltpu.VMEM((tiles, half, OUT_TILE), bf16),
            pltpu.SemaphoreType.DMA((3, SLOTS, heads)),
            pltpu.SemaphoreType.DMA((SLOTS, heads)),
            pltpu.SemaphoreType.DMA((3, SLOTS)),
            pltpu.SemaphoreType.DMA((SLOTS,)),
            pltpu.SemaphoreType.DMA,
            pltpu.SemaphoreType.DMA((tiles,)),
            pltpu.SemaphoreType.DMA((tiles,)),
        ],
        compiler_params=pltpu.CompilerParams(
            collective_id=0, has_side_effects=True, vmem_limit_bytes=60 * 1024 * 1024
        ),
    )(queries, key_matrix, value_matrix, doc_ids.reshape(1, tok), out_weight)


def solution(mesh):
    placed = (P("ctx", "head"), P("ctx", "head"), P("ctx", "head"), P("ctx"), P("head", None))
    neighbours = mesh.shape["ctx"] == 4 * PLANE and mesh.shape["head"] == 2
    return jax.shard_map(
        fused_device if neighbours else gathered_attention,
        mesh=mesh,
        in_specs=placed,
        out_specs=P(("ctx", "head"), None),
        check_vma=False,
    )
```

```python
import functools
import jax
import jax.numpy as jnp
from jax import lax
from jax.experimental import pallas as pl
from jax.experimental.pallas import tpu as pltpu
from jax.sharding import PartitionSpec as P

HEAD_WIDTH = 128


def gathered_attention(queries, key_matrix, value_matrix, doc_ids, out_weight):
    tok_rows = queries.shape[0]
    kv_here = key_matrix.shape[1] // HEAD_WIDTH
    queries_per_group = queries.shape[1] // key_matrix.shape[1]
    all_rows = queries_per_group * tok_rows
    my_index = lax.axis_index("ctx")
    q_pos = my_index * tok_rows + jnp.arange(tok_rows, dtype=jnp.int32)
    q_rows = (
        queries.reshape(tok_rows, kv_here, queries_per_group, HEAD_WIDTH)
        .transpose(1, 2, 0, 3)
        .reshape(kv_here, all_rows, HEAD_WIDTH)
    )
    score_scale = HEAD_WIDTH ** (-0.5)
    running = jnp.full((kv_here, all_rows), -1e30, jnp.float32)
    part_keys = lax.all_gather(key_matrix, "ctx", axis=0, tiled=True)
    part_values = lax.all_gather(value_matrix, "ctx", axis=0, tiled=True)
    part_docs = lax.all_gather(doc_ids, "ctx", axis=0, tiled=True)
    key_count = part_keys.shape[0]
    k_pos = jnp.arange(key_count, dtype=jnp.int32)
    keys_three = part_keys.reshape(key_count, kv_here, HEAD_WIDTH).transpose(1, 0, 2)
    values_three = part_values.reshape(key_count, kv_here, HEAD_WIDTH).transpose(1, 0, 2)
    scores = (
        jnp.einsum("hqd,hkd->hqk", q_rows, keys_three, preferred_element_type=jnp.float32)
        * score_scale
    )
    allowed = (
        (doc_ids[:, None] == part_docs[None, :])
        & (q_pos[:, None] >= k_pos[None, :])
        & (k_pos[None, :] >= 0)
    )
    allowed = jnp.tile(allowed, (queries_per_group, 1))[None]
    scores = jnp.where(allowed, scores, jnp.float32(-1e30))
    new_max = jnp.maximum(running, jnp.max(scores, axis=-1))
    weights = jnp.where(allowed, jnp.exp(scores - new_max[..., None]), jnp.float32(0.0))
    denominator = jnp.sum(weights, axis=-1)
    weighted = jnp.einsum(
        "hqk,hkd->hqd",
        weights.astype(jnp.bfloat16),
        values_three,
        preferred_element_type=jnp.float32,
    )
    running_state = (new_max, denominator, weighted)
    running, denominator, weighted = running_state
    attended = (weighted / denominator[..., None]).astype(jnp.bfloat16)
    attended = (
        attended.reshape(kv_here, queries_per_group, tok_rows, HEAD_WIDTH)
        .transpose(2, 0, 1, 3)
        .reshape(tok_rows, kv_here * queries_per_group * HEAD_WIDTH)
    )
    return lax.psum_scatter(
        jnp.dot(attended, out_weight, preferred_element_type=jnp.float32).astype(jnp.bfloat16),
        "head",
        scatter_dimension=0,
        tiled=True,
    )


NEG = -1e30
LOG2E = 1.4426950408889634
PLANE = 4
REACH = 9
SLOTS = REACH + 1
OUT_TILE = 512


def fused_kernel(
    q_ref, k_ref, v_ref, doc_ref, w_hbm, out_ref,
    kv, docs, flags, q_wide, k_wide, v_wide, m_s, acc, att, w_vm, total, theirs, swapped,
    send_sem, recv_sem, dsend_sem, drecv_sem, w_sem, osend_sem, orecv_sem,
):
    tok = q_ref.shape[0]
    heads = k_ref.shape[1] // HEAD_WIDTH
    group = q_ref.shape[1] // k_ref.shape[1]
    me = lax.axis_index("ctx")
    core = lax.axis_index("head")
    z, y, x = me // PLANE, (me // 2) % 2, me % 2
    dx, dy = 1 - 2 * x, 2 - 4 * y
    x_src = (4 * x, 4 + 4 * x, 2 + 4 * (1 - x) * (1 - y))
    y_src = (4 * y, 4 + 4 * y, 3 + 4 * y + x * (2 - 4 * y))
    z_src = (0, 4, 5)
    planes = lax.axis_size("ctx") // PLANE
    links = (
        (x_src, dx, None),
        (y_src, dy, None),
        (z_src, PLANE, z < planes - 1),
    )

    barrier = pltpu.get_barrier_semaphore()
    pl.semaphore_signal(barrier, inc=1, device_id={"ctx": me + dx})
    pl.semaphore_signal(barrier, inc=1, device_id={"ctx": me + dy})
    pl.semaphore_signal(barrier, inc=1, device_id={"head": 1 - core})

    @pl.when(z < planes - 1)
    def _():
        pl.semaphore_signal(barrier, inc=1, device_id={"ctx": me + PLANE})

    @pl.when(z > 0)
    def _():
        pl.semaphore_signal(barrier, inc=1, device_id={"ctx": me - PLANE})

    weight_copy = pltpu.make_async_copy(w_hbm, w_vm, w_sem)
    weight_copy.start()
    for h in range(heads):
        columns = pl.ds(h * HEAD_WIDTH, HEAD_WIDTH)
        kv[0, h, 0] = k_ref[:, columns]
        kv[0, h, 1] = v_ref[:, columns]
    docs[0] = jnp.broadcast_to(doc_ref[...], docs.shape[1:])


    peers = 3 + jnp.where(z > 0, 1, 0) + jnp.where(z < planes - 1, 1, 0)
    pl.semaphore_wait(barrier, peers)

    def chunk_copy(link, s, h, half):
        step = links[link][1]
        return pltpu.make_async_remote_copy(
            src_ref=kv.at[s, h, half],
            dst_ref=kv.at[s + step, h, half],
            send_sem=send_sem.at[link, s, h, half],
            recv_sem=recv_sem.at[s + step, h, half],
            device_id={"ctx": me + step},
        )

    def doc_copy(link, s):
        step = links[link][1]
        return pltpu.make_async_remote_copy(
            src_ref=docs.at[s],
            dst_ref=docs.at[s + step],
            send_sem=dsend_sem.at[link, s],
            recv_sem=drecv_sem.at[s + step],
            device_id={"ctx": me + step},
        )

    def sends(link, s, count=3):
        sources, _, also = links[link]
        here = s == sources[0]
        for i in range(1, count):
            here = here | (s == sources[i])
        if also is not None:
            here = here & also
        return here

    def start_send(link, s, h, half):
        if half == 0:
            @pl.when(h == 0)
            def _():
                doc_copy(link, s).start()

        chunk_copy(link, s, h, half).start()

    def forward(s, h, half):
        for link, count in ((2, 3), (0, 2), (1, 2)):
            @pl.when(sends(link, s, count))
            def _():
                start_send(link, s, h, half)

    def forward_last(h):
        for link in (0, 1):
            s = links[link][0][2]

            @pl.when(me >= s)
            def _():
                start_send(link, s, h, 0)
                start_send(link, s, h, 1)

    def send_own(h, carry):
        forward(jnp.int32(0), h, 0)
        forward(jnp.int32(0), h, 1)
        return carry

    lax.fori_loop(0, heads, send_own, 0)

    def blank(s, carry):
        docs[s] = jnp.full(docs.shape[1:], -1, jnp.int32)
        kv[s] = jnp.zeros(kv.shape[1:], kv.dtype)
        return carry

    lax.fori_loop(jnp.minimum(me + 1, SLOTS), SLOTS, blank, 0)

    score_scale = HEAD_WIDTH ** (-0.5) * LOG2E
    doc_rows = lax.broadcasted_iota(jnp.int32, (HEAD_WIDTH, tok), 0)

    def doc_columns(s, same, other):
        flags = jnp.where(docs[s, 0:1, :] == doc_rows, same, other).astype(jnp.float32)
        return flags.T.astype(jnp.bfloat16)

    own_docs = doc_columns(0, 1.0, 0.0)
    for r in range(group):
        q_wide[r, :, HEAD_WIDTH:] = own_docs
    v_wide[:, HEAD_WIDTH:] = jnp.ones((v_wide.shape[0], HEAD_WIDTH), jnp.bfloat16)

    def fill(j, s, h):
        @pl.when(h == 0)
        def _():
            flags[s] = doc_columns(s, 0.0, NEG)

        k_wide[j * tok:(j + 1) * tok, :HEAD_WIDTH] = kv[s, h, 0]
        k_wide[j * tok:(j + 1) * tok, HEAD_WIDTH:] = flags[s]
        v_wide[j * tok:(j + 1) * tok, :HEAD_WIDTH] = kv[s, h, 1]

    def piece(h, count, first):
        for r in range(group):
            place = pl.multiple_of((h * group + r) * HEAD_WIDTH, HEAD_WIDTH)
            q_wide[r, :, :HEAD_WIDTH] = q_ref[:, pl.ds(place, HEAD_WIDTH)]
        keys = k_wide[:count]
        values = v_wide[:count]

        def score(r):
            return lax.dot_general(
                q_wide[r], keys, (((1,), (1,)), ((), ())),
                preferred_element_type=jnp.float32,
            )

        upcoming = score(0)
        for r in range(group):
            scores = upcoming
            head = h * group + r
            if r + 1 < group:
                upcoming = score(r + 1)
            if first:
                rows = lax.broadcasted_iota(jnp.int32, (tok, tok), 0)
                cols = lax.broadcasted_iota(jnp.int32, (tok, tok), 1)
                scores = jnp.where(rows >= cols, scores, NEG)
            top = jnp.broadcast_to(
                jnp.max(scores, axis=1, keepdims=True), (tok, HEAD_WIDTH)
            )
            if not first:
                before = m_s[head]
                top = jnp.maximum(before, top)
            shift = jnp.concatenate([top * score_scale] * (count // HEAD_WIDTH), axis=1)
            weights = jnp.exp2(scores * score_scale - shift).astype(jnp.bfloat16)
            summed = jnp.dot(weights, values, preferred_element_type=jnp.float32)
            if not first:
                fade = jnp.exp2((before - top) * score_scale)
                summed = summed + acc[head] * jnp.concatenate([fade, fade], axis=1)
            m_s[head] = top
            acc[head] = summed

    turn = 3
    x_third = x * (7 - 4 * y) + (1 - x)
    y_third = x * (3 + 4 * y) + (1 - x) * 5

    def pick(place):
        z_slot = jnp.where(place < turn, 4, jnp.where(place < 2 * turn, 8, REACH))
        x_slot = jnp.where(place < turn, 3 - 2 * x, jnp.where(place < 2 * turn, 7 - 2 * x, x_third))
        y_slot = jnp.where(place < turn, 2, jnp.where(place < 2 * turn, 6, y_third))
        j = place % turn
        late = place >= 2 * turn
        first = jnp.where(late, x_slot, z_slot)
        second = jnp.where(late, y_slot, x_slot)
        third = jnp.where(late, z_slot, y_slot)
        return jnp.where(j == 0, first, jnp.where(j == 1, second, third))

    half = out_ref.shape[0]
    tiles = out_ref.shape[1] // OUT_TILE
    keep = pl.multiple_of(core * half, half)
    give = pl.multiple_of((1 - core) * half, half)
    span = group * HEAD_WIDTH

    def tile_columns(i):
        return pl.ds(pl.multiple_of(i * OUT_TILE, OUT_TILE), OUT_TILE)

    def swap_copy(i):
        return pltpu.make_async_remote_copy(
            src_ref=theirs.at[i],
            dst_ref=swapped.at[i],
            send_sem=osend_sem.at[i],
            recv_sem=orecv_sem.at[i],
            device_id={"head": 1 - core},
        )

    def project_head(h):
        for r in range(group):
            head = h * group + r
            att[:, r * HEAD_WIDTH:(r + 1) * HEAD_WIDTH] = (
                acc[head, :, :HEAD_WIDTH] / acc[head, :, HEAD_WIDTH:]
            ).astype(jnp.bfloat16)

        @pl.when(h == 0)
        def _():
            weight_copy.wait()

        weight_rows = pl.ds(pl.multiple_of(h * span, span), span)

        def project(i, inner):
            columns = tile_columns(i)
            share = jnp.dot(
                att[...], w_vm[weight_rows, columns], preferred_element_type=jnp.float32
            )

            @pl.when(h == 0)
            def _():
                total[:, columns] = share

            @pl.when(h > 0)
            def _():
                total[:, columns] += share

            @pl.when(h == heads - 1)
            def _():
                theirs[i] = total[pl.ds(give, half), columns].astype(jnp.bfloat16)
                swap_copy(i).start()

            return inner

        lax.fori_loop(0, tiles, project, 0)

    def own_piece(h):
        fill(0, 0, h)
        piece(h, tok, True)

    own_piece(jnp.int32(0))
    lag = heads + 2

    def arrive(t, carry):
        around = t // heads
        h = t % heads

        @pl.when((t >= lag) & (t < lag + heads))
        def _():
            forward_last(t - lag)

        for half in range(2):
            for j in range(turn):
                s = pick(around * turn + j)

                @pl.when(me >= s)
                def _():
                    landed = kv.at[s, h, half]
                    pltpu.make_async_copy(landed, landed, recv_sem.at[s, h, half]).wait()
                    if half == 0:
                        @pl.when(h == 0)
                        def _():
                            pltpu.make_async_copy(
                                docs.at[s], docs.at[s], drecv_sem.at[s]
                            ).wait()

                    forward(s, h, half)

        @pl.when(t < heads - 1)
        def _():
            own_piece(t + 1)

        for j in range(turn):
            fill(j, pick(around * turn + j), h)
        piece(h, turn * tok, False)

        @pl.when(around == REACH // turn - 1)
        def _():
            project_head(h)

        return carry

    lax.fori_loop(0, REACH // turn * heads, arrive, 0)

    def combine(i, carry):
        swap_copy(i).wait()
        columns = tile_columns(i)
        out_ref[:, columns] = (
            total[pl.ds(keep, half), columns] + swapped[i].astype(jnp.float32)
        ).astype(jnp.bfloat16)
        return carry

    lax.fori_loop(0, tiles, combine, 0)

    def settle(s, carry):
        for link in range(3):
            @pl.when(sends(link, s) & (me >= s))
            def _():
                doc_copy(link, s).wait_send()
                for h in range(heads):
                    for half in range(2):
                        chunk_copy(link, s, h, half).wait_send()
        return carry

    lax.fori_loop(0, SLOTS, settle, 0)


def fused_device(queries, key_matrix, value_matrix, doc_ids, out_weight):
    tok, width = queries.shape
    heads = key_matrix.shape[1] // HEAD_WIDTH
    group = width // key_matrix.shape[1]
    out_width = out_weight.shape[1]
    half = tok // 2
    tiles = out_width // OUT_TILE
    vmem = pl.BlockSpec(memory_space=pltpu.VMEM)
    f32, bf16 = jnp.float32, jnp.bfloat16
    return pl.pallas_call(
        fused_kernel,
        out_shape=jax.ShapeDtypeStruct((half, out_width), bf16),
        in_specs=[vmem] * 4 + [pl.BlockSpec(memory_space=pl.ANY)],
        out_specs=vmem,
        scratch_shapes=[
            pltpu.VMEM((SLOTS, heads, 2, tok, HEAD_WIDTH), bf16),
            pltpu.VMEM((SLOTS, 8, tok), jnp.int32),
            pltpu.VMEM((SLOTS, tok, HEAD_WIDTH), bf16),
            pltpu.VMEM((group, tok, 2 * HEAD_WIDTH), bf16),
            pltpu.VMEM((3 * tok, 2 * HEAD_WIDTH), bf16),
            pltpu.VMEM((3 * tok, 2 * HEAD_WIDTH), bf16),
            pltpu.VMEM((heads * group, tok, HEAD_WIDTH), f32),
            pltpu.VMEM((heads * group, tok, 2 * HEAD_WIDTH), f32),
            pltpu.VMEM((tok, group * HEAD_WIDTH), bf16),
            pltpu.VMEM(out_weight.shape, bf16),
            pltpu.VMEM((tok, out_width), f32),
            pltpu.VMEM((tiles, half, OUT_TILE), bf16),
            pltpu.VMEM((tiles, half, OUT_TILE), bf16),
            pltpu.SemaphoreType.DMA((3, SLOTS, heads, 2)),
            pltpu.SemaphoreType.DMA((SLOTS, heads, 2)),
            pltpu.SemaphoreType.DMA((3, SLOTS)),
            pltpu.SemaphoreType.DMA((SLOTS,)),
            pltpu.SemaphoreType.DMA,
            pltpu.SemaphoreType.DMA((tiles,)),
            pltpu.SemaphoreType.DMA((tiles,)),
        ],
        compiler_params=pltpu.CompilerParams(
            collective_id=0, has_side_effects=True, vmem_limit_bytes=60 * 1024 * 1024
        ),
    )(queries, key_matrix, value_matrix, doc_ids.reshape(1, tok), out_weight)


def solution(mesh):
    placed = (P("ctx", "head"), P("ctx", "head"), P("ctx", "head"), P("ctx"), P("head", None))
    neighbours = mesh.shape["ctx"] == 4 * PLANE and mesh.shape["head"] == 2
    return jax.shard_map(
        fused_device if neighbours else gathered_attention,
        mesh=mesh,
        in_specs=placed,
        out_specs=P(("ctx", "head"), None),
        check_vma=False,
    )
```
